32 devices in a mesh: hi: 2 (over y), lo: 16 (over z, x, core).
Axes of the slice: x: 2, y: 2, z: 4, core: 2. Of those that a mesh axis runs over, the one named last changes fastest.
Arguments:
- warm_start: float32 [256, 2, 256, 256], P(('hi', 'lo')), may hold values from -60 to 60
- h_blocks: float32 [4, 4, 64, 64], replicated, may hold values from -0.375 to 0.375
- block_mask: int32 [4, 4], replicated, may hold values 0 or 1
- coupling: float32 [8, 256, 256], replicated, may hold values from -0.09375 to 0.09375
- mode_block: int32 [8], replicated, may hold values from 0 to 3
- mode_of_bit: int32 [8], replicated, may hold values from 0 to 7, each once
- rates: float32 [8], replicated, may hold values from 0.3 to 3
- correlation_real: float32 [8], replicated, may hold values from 0.2 to 2
- correlation_imaginary: float32 [8], replicated, may hold values from -1 to 1
- dipole: float32 [256], replicated, may hold values from 0.5 to 2
- density: float32 [2, 256, 256], replicated, may hold values from -6 to 6
- frequency: float32 [1], replicated, may hold values from -2 to 2
- broadening: float32 [1], replicated, may hold values from 1 to 3
Outputs:
- solution: float32 [256, 2, 256, 256], P(('hi', 'lo'))
- residual: float32 [256, 2, 256, 256], P(('hi', 'lo'))
The draws below stay inside these ranges and needn't reach their ends.
Inputs may be any that keep to these rules, and one draw needn't show every extreme that they name: `mode_of_bit`: each of 0 to 7 appears once.
All inputs are finite; a program needn't handle non-finite values.
Results may differ from the reference program's by a relative error of at most 0.0003.
Values sent between devices are 32-bit elements; how exact they have to be, the bound alone decides.
A program may use at most 320 MiB of HBM per device.

```python
import math
import jax
import jax.numpy as jnp
from jax import lax

N = 256
BLOCK = 64
MODES = 8
NB = 4
AUX = 256


def draw_warm_start(key, part):
    first_key, row_key, col_key = jax.random.split(key, 3)
    shape = (AUX, 2, N, N)
    row_scale = jnp.exp(jax.random.uniform(row_key, (AUX, 1, N, 1), jnp.float32, 0.0, math.log(3.2)))
    col_scale = jnp.exp(jax.random.uniform(col_key, (AUX, 1, 1, N), jnp.float32, 0.0, math.log(3.2)))
    base = jnp.clip(jax.random.normal(first_key, shape, jnp.float32), -5.0, 5.0)
    return (base * row_scale * col_scale).astype(jnp.float32)


def place_ends(drawn, own_key, low, high):
    index_at = [jax.random.randint(jax.random.fold_in(own_key, axis), (), 0, length) for axis, length in enumerate(drawn.shape)]
    main_axis = drawn.shape.index(max(drawn.shape))
    next_to = index_at[:main_axis] + [(index_at[main_axis] + 1) % drawn.shape[main_axis]] + index_at[main_axis + 1:]
    return drawn.at[tuple(index_at)].set(low).at[tuple(next_to)].set(high)


def gaussian(key, dims, scale, bound, held_as=jnp.bfloat16):
    array = scale * jax.random.normal(key, dims, jnp.float32)
    return jnp.clip(array, min=-bound, max=bound).astype(held_as)


def setup_inputs(seed: int = 0) -> dict:
    keys = jax.random.split(jax.random.key(seed), 14)
    return {
        "warm_start": draw_warm_start(jax.random.fold_in(keys[13], 71), 0),
        "h_blocks": gaussian(keys[1], (NB, NB, BLOCK, BLOCK), N ** -0.5, 0.375, jnp.float32),
        "block_mask": place_ends((jax.random.randint(keys[2], (NB, NB), 0, 2) < 1).astype(jnp.int32), jax.random.fold_in(keys[2], 1), 0, 1),
        "coupling": gaussian(keys[3], (MODES, N, N), (16 * N) ** -0.5, 0.09375, jnp.float32),
        "mode_block": place_ends(jax.random.randint(keys[4], (MODES,), 0, NB), jax.random.fold_in(keys[4], 1), 0, NB - 1).astype(jnp.int32),
        "mode_of_bit": jax.random.permutation(keys[5], MODES).astype(jnp.int32),
        "rates": jnp.clip(jnp.exp(jax.random.uniform(keys[6], (MODES,), jnp.float32, math.log(0.3), math.log(3.0))), 0.3, 3.0),
        "correlation_real": jnp.clip(jnp.exp(jax.random.uniform(keys[7], (MODES,), jnp.float32, math.log(0.2), math.log(2.0))), 0.2, 2.0),
        "correlation_imaginary": jnp.clip(jax.random.uniform(keys[8], (MODES,), jnp.float32, -1.0, 1.0), -1.0, 1.0),
        "dipole": jnp.clip(jax.random.uniform(keys[9], (N,), jnp.float32, 0.5, 2.0), 0.5, 2.0),
        "density": gaussian(keys[10], (2, N, N), 1.0, 6.0, jnp.float32),
        "frequency": jnp.clip(jax.random.uniform(keys[11], (1,), jnp.float32, -2.0, 2.0), -2.0, 2.0),
        "broadening": jnp.clip(jnp.exp(jax.random.uniform(keys[12], (1,), jnp.float32, math.log(1.0), math.log(3.0))), 1.0, 3.0),
    }


FULL_PRECISION = lax.Precision.HIGHEST
SITE_STRENGTH = 0.5


def left_multiplied(matrix, probe_field):
    return jnp.einsum("ij,apjk->apik", matrix, probe_field, precision=FULL_PRECISION)


def right_multiplied(probe_field, matrix):
    return jnp.einsum("apij,jk->apik", probe_field, matrix, precision=FULL_PRECISION)


def rotate_quarter(probe_field):
    return jnp.stack([-probe_field[:, 1], probe_field[:, 0]], axis=1)


def scale_complex(real_part, imag_part, probe_field):
    return jnp.stack([real_part * probe_field[:, 0] - imag_part * probe_field[:, 1],
                      real_part * probe_field[:, 1] + imag_part * probe_field[:, 0]], axis=1)


def inner_terms(first, second):
    real_part = jnp.sum(first * second)
    imag_part = jnp.sum(first[:, 0] * second[:, 1] - first[:, 1] * second[:, 0])
    return real_part, imag_part


def complex_ratio(top_re, top_im, low_re, low_im):
    modulus = low_re * low_re + low_im * low_im
    return (top_re * low_re + top_im * low_im) / modulus, (top_im * low_re - top_re * low_im) / modulus


def build_hamiltonian(h_blocks, block_mask):
    count = h_blocks.shape[0]
    width = h_blocks.shape[2]
    masked = h_blocks * block_mask.astype(h_blocks.dtype)[:, :, None, None]
    whole = jnp.transpose(masked, (0, 2, 1, 3)).reshape(count * width, count * width)
    return 0.5 * (whole + whole.T)


def build_couplings(coupling, mode_block, width):
    states = coupling.shape[1]
    symmetric = 0.5 * (coupling + jnp.swapaxes(coupling, 1, 2))
    owner = jnp.arange(states, dtype=jnp.int32) // width
    onsite = (owner[None, :] == mode_block[:, None]).astype(coupling.dtype) * SITE_STRENGTH
    return symmetric + jnp.eye(states, dtype=coupling.dtype)[None] * onsite[:, None, :]


def coupling_terms_list(neighbour_index, coupling_matrix, single_bit_value, mode_coefficient_real, mode_coefficient_imag):
    left_portion = left_multiplied(coupling_matrix, neighbour_index)
    right_portion = right_multiplied(neighbour_index, coupling_matrix)
    lower = (1.0 - single_bit_value)[:, None, None, None]
    upper = single_bit_value[:, None, None, None]
    raising = rotate_quarter(left_portion - right_portion)
    lowering = rotate_quarter(scale_complex(mode_coefficient_real, mode_coefficient_imag, left_portion) - scale_complex(mode_coefficient_real, -mode_coefficient_imag, right_portion))
    lowering_adj = rotate_quarter(scale_complex(mode_coefficient_real, -mode_coefficient_imag, left_portion) - scale_complex(mode_coefficient_real, mode_coefficient_imag, right_portion))
    forward = lower * raising + upper * lowering
    adjoint = -upper * raising - lower * lowering_adj
    return forward, adjoint


def apply_forward_adjoint(probe_field, hamiltonian_matrix, coupling_matrices, decay_rate_bits, real_bit_set, imaginary_bit_set, angular_frequency, damping_offset):
    count = probe_field.shape[0]
    index = jnp.arange(count, dtype=jnp.int32)
    damping = damping_offset + jnp.zeros((count,), probe_field.dtype)
    entry_values = []
    for selector_flag in range(MODES):
        value = ((index // (2 ** selector_flag)) % 2).astype(probe_field.dtype)
        entry_values.append(value)
        damping = damping + value * decay_rate_bits[selector_flag]
    spread = damping[:, None, None, None] * probe_field
    commutator = rotate_quarter(angular_frequency * probe_field + left_multiplied(hamiltonian_matrix, probe_field) - right_multiplied(probe_field, hamiltonian_matrix))
    forward = spread + commutator
    adjoint = spread - commutator
    for selector_flag in range(MODES):
        shaped = probe_field.reshape((count // 2 ** (selector_flag + 1), 2, 2 ** selector_flag) + probe_field.shape[1:])
        neighbour_index = jnp.flip(shaped, axis=1).reshape(probe_field.shape)
        additional_forward, additional_adjoint = coupling_terms_list(neighbour_index, coupling_matrices[selector_flag], entry_values[selector_flag], real_bit_set[selector_flag], imaginary_bit_set[selector_flag])
        forward = forward + additional_forward
        adjoint = adjoint + additional_adjoint
    return forward, adjoint


def reference(warm_start, h_blocks, block_mask, coupling, mode_block, mode_of_bit, rates, correlation_real, correlation_imaginary, dipole, density, frequency, broadening):
    hamiltonian_matrix = build_hamiltonian(h_blocks, block_mask)
    stacked_couplings = build_couplings(coupling, mode_block, h_blocks.shape[2])
    coupling_matrices = stacked_couplings[mode_of_bit]
    decay_rate_bits = rates[mode_of_bit]
    real_bit_set = correlation_real[mode_of_bit]
    imaginary_bit_set = correlation_imaginary[mode_of_bit]
    angular_frequency = frequency[0]
    damping_offset = broadening[0]

    def operate(probe_field):
        return apply_forward_adjoint(probe_field, hamiltonian_matrix, coupling_matrices, decay_rate_bits, real_bit_set, imaginary_bit_set, angular_frequency, damping_offset)

    source = jnp.zeros_like(warm_start).at[0].set(dipole[None, :, None] * density)
    image_start, unused_adj = operate(warm_start)
    start_resid = source - image_start
    start_norm = jnp.sum(start_resid * start_resid)
    probe, probe_adj = operate(start_resid)
    curve_re, curve_im = inner_terms(start_resid, probe)
    alpha_re, alpha_im = complex_ratio(start_norm, 0.0, curve_re, curve_im)
    first_iterate = warm_start + scale_complex(alpha_re, alpha_im, start_resid)
    next_resid = start_resid - scale_complex(alpha_re, alpha_im, probe)
    shadow = start_resid - scale_complex(alpha_re, -alpha_im, probe_adj)
    rho_re, rho_im = inner_terms(shadow, next_resid)
    beta_re = rho_re / start_norm
    beta_im = rho_im / start_norm
    direction = next_resid + scale_complex(beta_re, beta_im, start_resid)
    shadow_dir = shadow + scale_complex(beta_re, -beta_im, start_resid)
    image, unused_second = operate(direction)
    next_re, next_im = inner_terms(shadow_dir, image)
    step_re, step_im = complex_ratio(rho_re, rho_im, next_re, next_im)
    solution = first_iterate + scale_complex(step_re, step_im, direction)
    residual = next_resid - scale_complex(step_re, step_im, image)
    return solution, residual
```

```python
import functools

import jax
import jax.numpy as jnp
from jax import lax
from jax.experimental import pallas as pl
from jax.experimental.pallas import tpu as pltpu
from jax.sharding import PartitionSpec as P

SITE_STRENGTH = 0.5


def complex_ratio(top_re, top_im, low_re, low_im):
    modulus = low_re * low_re + low_im * low_im
    return (
        (top_re * low_re + top_im * low_im) / modulus,
        (top_im * low_re - top_re * low_im) / modulus,
    )


def product(a_re, a_im, b_re, b_im):
    return a_re * b_re - a_im * b_im, a_re * b_im + a_im * b_re


def build_hamiltonian(h_blocks, block_mask):
    count = h_blocks.shape[0]
    width = h_blocks.shape[2]
    masked = h_blocks * block_mask.astype(h_blocks.dtype)[:, :, None, None]
    whole = jnp.transpose(masked, (0, 2, 1, 3)).reshape(count * width, count * width)
    return 0.5 * (whole + whole.T)


def build_couplings(coupling, mode_block, width):
    states = coupling.shape[1]
    symmetric = 0.5 * (coupling + jnp.swapaxes(coupling, 1, 2))
    owner = jnp.arange(states, dtype=jnp.int32) // width
    onsite = (owner[None, :] == mode_block[:, None]).astype(coupling.dtype) * SITE_STRENGTH
    return symmetric + jnp.eye(states, dtype=coupling.dtype)[None] * onsite[:, None, :]


def split(value):
    high = value.astype(jnp.bfloat16)
    low = (value - high.astype(jnp.float32)).astype(jnp.bfloat16)
    return high, low


def apply_kernel(kind, terms, table, left_ref, right_ref, *refs):
    fields = refs[:terms]
    if kind == "start":
        source, refs = refs[terms], refs[terms + 1 :]
    else:
        refs = refs[terms:]
    out = refs[0]
    row = pl.program_id(0)
    n = out.shape[-1]
    damping = table[row, 0]
    frequency = table[row, 1]
    y_re, y_im = fields[0][0, 0], fields[0][0, 1]
    f_re, f_im = frequency * y_re, frequency * y_im
    g_re, g_im = f_re, f_im
    for t in range(terms):
        e_re, e_im = table[row, 4 + 4 * t], table[row, 5 + 4 * t]
        h_re, h_im = table[row, 6 + 4 * t], table[row, 7 + 4 * t]
        re_high, re_low = split(fields[t][0, 0])
        im_high, im_low = split(fields[t][0, 1])
        high = jnp.concatenate([re_high, im_high], axis=1)
        low = jnp.concatenate([re_low, im_low], axis=1)
        stacked = jnp.concatenate([high, low, high], axis=0)
        left = jnp.dot(left_ref[t], stacked, preferred_element_type=jnp.float32)
        high = jnp.concatenate([re_high, im_high], axis=0)
        low = jnp.concatenate([re_low, im_low], axis=0)
        stacked = jnp.concatenate([high, low, high], axis=1)
        right = jnp.dot(stacked, right_ref[t], preferred_element_type=jnp.float32)
        d_re = left[:, :n] - right[:n]
        d_im = left[:, n:] - right[n:]
        if t == 0:
            f_re, f_im = f_re + d_re, f_im + d_im
            if kind == "both":
                g_re, g_im = f_re, f_im
            continue
        s_re = left[:, :n] + right[:n]
        s_im = left[:, n:] + right[n:]
        f_re = f_re + (e_re * d_re - e_im * s_im)
        f_im = f_im + (e_re * d_im + e_im * s_re)
        if kind == "both":
            g_re = g_re + (h_re * d_re - h_im * s_im)
            g_im = g_im + (h_re * d_im + h_im * s_re)
    a_re = damping * y_re - f_im
    a_im = damping * y_im + f_re
    if kind == "start":
        flag = table[row, 2]
        out[0, 0] = flag * source[0] - a_re
        out[0, 1] = flag * source[1] - a_im
        return
    out[0, 0] = a_re
    out[0, 1] = a_im
    if kind == "both":
        refs[1][0, 0] = damping * y_re + g_im
        refs[1][0, 1] = damping * y_im - g_re


def apply(kind, table, left, right, fields, flips, source=None):
    size, _, n, _ = fields[0].shape
    terms = len(fields)
    block = (1, 2, n, n)

    def flipped(flip):
        return pl.BlockSpec(block, lambda i: (i ^ flip, 0, 0, 0))

    once = pl.BlockSpec
    in_specs = [
        pl.BlockSpec(memory_space=pltpu.SMEM),
        once(left.shape, lambda i: (0, 0, 0)),
        once(right.shape, lambda i: (0, 0, 0)),
    ] + [flipped(flip) for flip in flips]
    operands = [table, left, right, *fields]
    if kind == "start":
        in_specs.append(once(source.shape, lambda i: (0, 0, 0)))
        operands.append(source)
    outs = 2 if kind == "both" else 1
    shape = jax.ShapeDtypeStruct(fields[0].shape, jnp.float32)
    return pl.pallas_call(
        functools.partial(apply_kernel, kind, terms),
        grid=(size,),
        in_specs=in_specs,
        out_specs=[flipped(0)] * outs,
        out_shape=[shape] * outs,
        compiler_params=pltpu.CompilerParams(vmem_limit_bytes=48 * 2**20),
        cost_estimate=pl.CostEstimate(
            flops=size * terms * 24 * n**3,
            bytes_accessed=(terms + outs) * size * 8 * n * n,
            transcendentals=0,
        ),
    )(*operands)


def on_device(
    warm_start,
    h_blocks,
    block_mask,
    coupling,
    mode_block,
    mode_of_bit,
    rates,
    correlation_real,
    correlation_imaginary,
    dipole,
    density,
    frequency,
    broadening,
):
    count = warm_start.shape[0]
    size = max(1, count // 4)
    chunks = count // size
    local_bits = count.bit_length() - 1
    inner_bits = size.bit_length() - 1
    lo_bits = lax.axis_size("lo").bit_length() - 1
    hi_bits = lax.axis_size("hi").bit_length() - 1
    bits = local_bits + lo_bits + hi_bits

    hamiltonian = build_hamiltonian(h_blocks, block_mask)
    stacked = build_couplings(coupling, mode_block, h_blocks.shape[2])
    couplings = jnp.stack(
        [lax.dynamic_index_in_dim(stacked, mode_of_bit[b], 0, keepdims=False) for b in range(bits)]
    )
    matrices = jnp.concatenate([hamiltonian[None], couplings], axis=0)
    kept = lax.reduce_precision(matrices, exponent_bits=8, mantissa_bits=7)
    high = kept.astype(jnp.bfloat16)
    low = (matrices - kept).astype(jnp.bfloat16)
    left = jnp.concatenate([high, high, low], axis=2)
    right = jnp.concatenate([high, high, low], axis=1)

    place = lax.axis_index("hi") * lax.axis_size("lo") + lax.axis_index("lo")
    index = place * count + jnp.arange(count, dtype=jnp.int32)
    level = ((index[:, None] >> jnp.arange(bits, dtype=jnp.int32)[None]) & 1).astype(jnp.float32)
    modes = jnp.arange(rates.shape[0], dtype=jnp.int32)
    chosen = mode_of_bit[:, None] == modes[None]

    def by_bit(values):
        return jnp.sum(jnp.where(chosen, values[None], 0.0), axis=1)[None]

    c_re = by_bit(correlation_real)
    c_im = by_bit(correlation_imaginary)
    damping = broadening[0] + jnp.sum(level * by_bit(rates), axis=1)
    factors = jnp.stack(
        [
            1.0 - level + level * c_re,
            level * c_im,
            level + (1.0 - level) * c_re,
            -(1.0 - level) * c_im,
        ],
        axis=2,
    ).reshape(count, 4 * bits)
    head = jnp.stack(
        [
            damping,
            jnp.zeros_like(damping) + frequency[0],
            (index == 0).astype(jnp.float32),
            jnp.zeros_like(damping),
            jnp.ones_like(damping),
            jnp.zeros_like(damping),
            jnp.ones_like(damping),
            jnp.zeros_like(damping),
        ],
        axis=1,
    )
    table = jnp.concatenate([head, factors], axis=1)
    source = dipole[None, :, None] * density

    def exchanged(piece):
        got = []
        for axis, axis_bits in (("lo", lo_bits), ("hi", hi_bits)):
            for bit in range(axis_bits):
                pairs = [(s, s ^ 2**bit) for s in range(lax.axis_size(axis))]
                got.append(lax.ppermute(piece, axis, pairs))
        return got

    def operate(kind, pieces):
        results = []
        remote = [exchanged(piece) for piece in pieces]
        for c in range(chunks):
            fields, flips = [pieces[c]], [0]
            for bit in range(local_bits):
                if bit < inner_bits:
                    fields.append(pieces[c])
                    flips.append(2**bit)
                else:
                    fields.append(pieces[c ^ 2 ** (bit - inner_bits)])
                    flips.append(0)
            fields += remote[c]
            flips += [0] * len(remote[c])
            rows = table[c * size : (c + 1) * size]
            results.append(apply(kind, rows, left, right, fields, flips, source))
        return [list(column) for column in zip(*results)]

    def inner(first, second):
        real, imag = 0.0, 0.0
        for u, z in zip(first, second):
            real += jnp.sum(u * z)
            imag += jnp.sum(u[:, 0] * z[:, 1] - u[:, 1] * z[:, 0])
        return real, imag

    x = [warm_start[c * size : (c + 1) * size] for c in range(chunks)]
    (r,) = operate("start", x)
    p, pa = operate("both", r)
    (q,) = operate("forward", p)
    norm = sum(jnp.sum(piece * piece) for piece in r)
    moments = jnp.stack([norm, *inner(r, p), *inner(pa, p), *inner(pa, q)])
    m0, m1r, m1i, m2r, m2i, m3r, m3i = lax.psum(moments, ("hi", "lo"))
    ar, ai = complex_ratio(m0, 0.0, m1r, m1i)
    a2r, a2i = product(ar, ai, ar, ai)
    t_re, t_im = product(a2r, a2i, m2r, m2i)
    rho_re, rho_im = t_re - m0, t_im
    br, bi = 1.0 + rho_re / m0, rho_im / m0
    b2r, b2i = product(br, bi, br, bi)
    abr, abi = product(ar, ai, br, bi)
    u_re, u_im = product(b2r, b2i, m1r, m1i)
    v_re, v_im = product(abr, abi, m2r, m2i)
    w_re, w_im = product(a2r, a2i, m3r, m3i)
    sr, si = complex_ratio(rho_re, rho_im, u_re - 2.0 * v_re + w_re, u_im - 2.0 * v_im + w_im)
    sbr, sbi = product(sr, si, br, bi)
    k_re, k_im = ar + sbr, ai + sbi
    l_re, l_im = product(sr, si, ar, ai)

    def blend(base, first, second):
        return jnp.stack(
            [
                base[:, 0] + (k_re * first[:, 0] - k_im * first[:, 1])
                - (l_re * second[:, 0] - l_im * second[:, 1]),
                base[:, 1] + (k_re * first[:, 1] + k_im * first[:, 0])
                - (l_re * second[:, 1] + l_im * second[:, 0]),
            ],
            axis=1,
        )

    answer = [blend(u, v, w) for u, v, w in zip(x, r, p)]
    rest = [blend(u, -v, -w) for u, v, w in zip(r, p, q)]
    return jnp.concatenate(answer, axis=0), jnp.concatenate(rest, axis=0)


def solution(mesh):
    spread = P(("hi", "lo"), None, None, None)
    return jax.shard_map(
        on_device,
        mesh=mesh,
        in_specs=(spread,) + (P(),) * 12,
        out_specs=(spread, spread),
        check_vma=False,
    )
```

```python
import functools

import jax
import jax.numpy as jnp
from jax import lax
from jax.experimental import pallas as pl
from jax.experimental.pallas import tpu as pltpu
from jax.sharding import PartitionSpec as P

SITE_STRENGTH = 0.5


def complex_ratio(top_re, top_im, low_re, low_im):
    modulus = low_re * low_re + low_im * low_im
    return (
        (top_re * low_re + top_im * low_im) / modulus,
        (top_im * low_re - top_re * low_im) / modulus,
    )


def product(a_re, a_im, b_re, b_im):
    return a_re * b_re - a_im * b_im, a_re * b_im + a_im * b_re


def build_hamiltonian(h_blocks, block_mask):
    count = h_blocks.shape[0]
    width = h_blocks.shape[2]
    masked = h_blocks * block_mask.astype(h_blocks.dtype)[:, :, None, None]
    whole = jnp.transpose(masked, (0, 2, 1, 3)).reshape(count * width, count * width)
    return 0.5 * (whole + whole.T)


def build_couplings(coupling, mode_block, width):
    states = coupling.shape[1]
    symmetric = 0.5 * (coupling + jnp.swapaxes(coupling, 1, 2))
    owner = jnp.arange(states, dtype=jnp.int32) // width
    onsite = (owner[None, :] == mode_block[:, None]).astype(coupling.dtype) * SITE_STRENGTH
    return symmetric + jnp.eye(states, dtype=coupling.dtype)[None] * onsite[:, None, :]


def split(value):
    high = value.astype(jnp.bfloat16)
    low = (value - high.astype(jnp.float32)).astype(jnp.bfloat16)
    return high, low


def apply_kernel(kind, terms, table, left_ref, right_ref, *refs):
    fields = refs[:terms]
    if kind == "start":
        source, refs = refs[terms], refs[terms + 1 :]
    else:
        refs = refs[terms:]
    out = refs[0]
    row = pl.program_id(0)
    n = out.shape[-1]
    damping = table[row, 0]
    frequency = table[row, 1]
    y_re, y_im = fields[0][0, 0], fields[0][0, 1]
    f_re, f_im = frequency * y_re, frequency * y_im
    g_re, g_im = f_re, f_im
    for t in range(terms):
        e_re, e_im = table[row, 4 + 4 * t], table[row, 5 + 4 * t]
        h_re, h_im = table[row, 6 + 4 * t], table[row, 7 + 4 * t]
        re_high, re_low = split(fields[t][0, 0])
        im_high, im_low = split(fields[t][0, 1])
        high = jnp.concatenate([re_high, im_high], axis=1)
        low = jnp.concatenate([re_low, im_low], axis=1)
        stacked = jnp.concatenate([high, low, high], axis=0)
        left = jnp.dot(left_ref[t], stacked, preferred_element_type=jnp.float32)
        high = jnp.concatenate([re_high, im_high], axis=0)
        low = jnp.concatenate([re_low, im_low], axis=0)
        stacked = jnp.concatenate([high, low, high], axis=1)
        right = jnp.dot(stacked, right_ref[t], preferred_element_type=jnp.float32)
        d_re = left[:, :n] - right[:n]
        d_im = left[:, n:] - right[n:]
        if t == 0:
            f_re, f_im = f_re + d_re, f_im + d_im
            if kind == "both":
                g_re, g_im = f_re, f_im
            continue
        s_re = left[:, :n] + right[:n]
        s_im = left[:, n:] + right[n:]
        f_re = f_re + (e_re * d_re - e_im * s_im)
        f_im = f_im + (e_re * d_im + e_im * s_re)
        if kind == "both":
            g_re = g_re + (h_re * d_re - h_im * s_im)
            g_im = g_im + (h_re * d_im + h_im * s_re)
    a_re = damping * y_re - f_im
    a_im = damping * y_im + f_re
    if kind == "start":
        flag = table[row, 2]
        out[0, 0] = flag * source[0] - a_re
        out[0, 1] = flag * source[1] - a_im
        return
    out[0, 0] = a_re
    out[0, 1] = a_im
    if kind == "both":
        refs[1][0, 0] = damping * y_re + g_im
        refs[1][0, 1] = damping * y_im - g_re


def apply(kind, table, left, right, fields, flips, source=None):
    size, _, n, _ = fields[0].shape
    terms = len(fields)
    block = (1, 2, n, n)

    def flipped(flip):
        return pl.BlockSpec(block, lambda i: (i ^ flip, 0, 0, 0))

    once = pl.BlockSpec
    in_specs = [
        pl.BlockSpec(memory_space=pltpu.SMEM),
        once(left.shape, lambda i: (0, 0, 0)),
        once(right.shape, lambda i: (0, 0, 0)),
    ] + [flipped(flip) for flip in flips]
    operands = [table, left, right, *fields]
    if kind == "start":
        in_specs.append(once(source.shape, lambda i: (0, 0, 0)))
        operands.append(source)
    outs = 2 if kind == "both" else 1
    shape = jax.ShapeDtypeStruct(fields[0].shape, jnp.float32)
    return pl.pallas_call(
        functools.partial(apply_kernel, kind, terms),
        grid=(size,),
        in_specs=in_specs,
        out_specs=[flipped(0)] * outs,
        out_shape=[shape] * outs,
        compiler_params=pltpu.CompilerParams(vmem_limit_bytes=48 * 2**20),
        cost_estimate=pl.CostEstimate(
            flops=size * terms * 24 * n**3,
            bytes_accessed=(terms + outs) * size * 8 * n * n,
            transcendentals=0,
        ),
    )(*operands)


def on_device(
    warm_start,
    h_blocks,
    block_mask,
    coupling,
    mode_block,
    mode_of_bit,
    rates,
    correlation_real,
    correlation_imaginary,
    dipole,
    density,
    frequency,
    broadening,
):
    count = warm_start.shape[0]
    size = max(1, count // 4)
    chunks = count // size
    local_bits = count.bit_length() - 1
    inner_bits = size.bit_length() - 1
    lo_bits = lax.axis_size("lo").bit_length() - 1
    hi_bits = lax.axis_size("hi").bit_length() - 1
    bits = local_bits + lo_bits + hi_bits

    hamiltonian = build_hamiltonian(h_blocks, block_mask)
    stacked = build_couplings(coupling, mode_block, h_blocks.shape[2])
    couplings = jnp.stack(
        [lax.dynamic_index_in_dim(stacked, mode_of_bit[b], 0, keepdims=False) for b in range(bits)]
    )
    matrices = jnp.concatenate([hamiltonian[None], couplings], axis=0)
    kept = lax.reduce_precision(matrices, exponent_bits=8, mantissa_bits=7)
    high = kept.astype(jnp.bfloat16)
    low = (matrices - kept).astype(jnp.bfloat16)
    left = jnp.concatenate([high, high, low], axis=2)
    right = jnp.concatenate([high, high, low], axis=1)

    place = lax.axis_index("hi") * lax.axis_size("lo") + lax.axis_index("lo")
    index = place * count + jnp.arange(count, dtype=jnp.int32)
    level = ((index[:, None] >> jnp.arange(bits, dtype=jnp.int32)[None]) & 1).astype(jnp.float32)
    modes = jnp.arange(rates.shape[0], dtype=jnp.int32)
    chosen = mode_of_bit[:, None] == modes[None]

    def by_bit(values):
        return jnp.sum(jnp.where(chosen, values[None], 0.0), axis=1)[None]

    c_re = by_bit(correlation_real)
    c_im = by_bit(correlation_imaginary)
    damping = broadening[0] + jnp.sum(level * by_bit(rates), axis=1)
    factors = jnp.stack(
        [
            1.0 - level + level * c_re,
            level * c_im,
            level + (1.0 - level) * c_re,
            -(1.0 - level) * c_im,
        ],
        axis=2,
    ).reshape(count, 4 * bits)
    head = jnp.stack(
        [
            damping,
            jnp.zeros_like(damping) + frequency[0],
            (index == 0).astype(jnp.float32),
            jnp.zeros_like(damping),
            jnp.ones_like(damping),
            jnp.zeros_like(damping),
            jnp.ones_like(damping),
            jnp.zeros_like(damping),
        ],
        axis=1,
    )
    table = jnp.concatenate([head, factors], axis=1)
    source = dipole[None, :, None] * density

    def partner(value, axis, bit):
        pairs = [(s, s ^ 2**bit) for s in range(lax.axis_size(axis))]
        return lax.ppermute(value, axis, pairs)

    def exchanged(piece):
        got = [partner(piece, "lo", bit) for bit in range(lo_bits)]
        return got + [partner(piece, "hi", bit) for bit in range(hi_bits)]

    def operate(kind, pieces):
        results = []
        remote = [exchanged(piece) for piece in pieces]
        for c in range(chunks):
            fields, flips = [pieces[c]], [0]
            for bit in range(local_bits):
                if bit < inner_bits:
                    fields.append(pieces[c])
                    flips.append(2**bit)
                else:
                    fields.append(pieces[c ^ 2 ** (bit - inner_bits)])
                    flips.append(0)
            fields += remote[c]
            flips += [0] * len(remote[c])
            rows = table[c * size : (c + 1) * size]
            results.append(apply(kind, rows, left, right, fields, flips, source))
        return [list(column) for column in zip(*results)]

    def inner(first, second):
        real, imag = 0.0, 0.0
        for u, z in zip(first, second):
            real += jnp.sum(u * z)
            imag += jnp.sum(u[:, 0] * z[:, 1] - u[:, 1] * z[:, 0])
        return real, imag

    x = [warm_start[c * size : (c + 1) * size] for c in range(chunks)]
    (r,) = operate("start", x)
    p, pa = operate("both", r)
    (q,) = operate("forward", p)
    norm = sum(jnp.sum(piece * piece) for piece in r)
    moments = jnp.stack([norm, *inner(r, p), *inner(pa, p), *inner(pa, q)])
    for axis, axis_bits in (("lo", lo_bits), ("hi", hi_bits)):
        for bit in range(axis_bits):
            moments = moments + partner(moments, axis, bit)
    m0, m1r, m1i, m2r, m2i, m3r, m3i = moments
    ar, ai = complex_ratio(m0, 0.0, m1r, m1i)
    a2r, a2i = product(ar, ai, ar, ai)
    t_re, t_im = product(a2r, a2i, m2r, m2i)
    rho_re, rho_im = t_re - m0, t_im
    br, bi = 1.0 + rho_re / m0, rho_im / m0
    b2r, b2i = product(br, bi, br, bi)
    abr, abi = product(ar, ai, br, bi)
    u_re, u_im = product(b2r, b2i, m1r, m1i)
    v_re, v_im = product(abr, abi, m2r, m2i)
    w_re, w_im = product(a2r, a2i, m3r, m3i)
    sr, si = complex_ratio(rho_re, rho_im, u_re - 2.0 * v_re + w_re, u_im - 2.0 * v_im + w_im)
    sbr, sbi = product(sr, si, br, bi)
    k_re, k_im = ar + sbr, ai + sbi
    l_re, l_im = product(sr, si, ar, ai)

    def blend(base, first, second):
        return jnp.stack(
            [
                base[:, 0] + (k_re * first[:, 0] - k_im * first[:, 1])
                - (l_re * second[:, 0] - l_im * second[:, 1]),
                base[:, 1] + (k_re * first[:, 1] + k_im * first[:, 0])
                - (l_re * second[:, 1] + l_im * second[:, 0]),
            ],
            axis=1,
        )

    answer = [blend(u, v, w) for u, v, w in zip(x, r, p)]
    rest = [blend(u, -v, -w) for u, v, w in zip(r, p, q)]
    return jnp.concatenate(answer, axis=0), jnp.concatenate(rest, axis=0)


def solution(mesh):
    spread = P(("hi", "lo"), None, None, None)
    return jax.shard_map(
        on_device,
        mesh=mesh,
        in_specs=(spread,) + (P(),) * 12,
        out_specs=(spread, spread),
        check_vma=False,
    )
```
